256 devices in a mesh: ctx: 32 (over y, z), head: 8 (over x, core).
Axes of the slice: x: 4, y: 4, z: 8, core: 2. Of those that a mesh axis runs over, the one named last changes fastest.
Arguments:
- queries: bfloat16 [32768, 4096], P('ctx', 'head'), may hold values from -6 to 6
- keys: bfloat16 [32768, 4096], P('ctx', 'head'), may hold values from -0.5 to 0.5
- values: bfloat16 [32768, 2048], P('ctx', 'head'), may hold values from -120 to 120
- norm_gain: bfloat16 [2048], P('head'), may hold values from 0.099609375 to 1.8984375
- level_index: int32 [10, 32, 32768], P(None, 'head', 'ctx'), may hold values from 1 to 256
Outputs:
- attended: bfloat16 [32768, 2048], P('ctx', 'head')
The draws below stay inside these ranges and needn't reach their ends.
All inputs are finite; a program needn't handle non-finite values.
Results may differ from the reference program's by a relative error of at most 0.0049.
Values sent between devices are 32-bit elements; how exact they have to be, the bound alone decides.
No kernel may reach another device: no remote copies, remote signals or barrier semaphores. Data moves between devices by JAX's collectives and lax.ppermute only.
A program may use at most 64 MiB of HBM per device.

```python
import jax
import jax.numpy as jnp
from jax import lax

H = 32
DK = 128
DV = 64
STRETCH = 64
STRETCH_BITS = 4
CTX_BITS = 5
LEV = 10
TOKENS = 32768


def draw_values(key, part):
    key = jax.random.fold_in(key, 11)
    base_key, row_key = jax.random.split(key)
    column = (jnp.arange(H * DV) // DV).astype(jnp.float32)
    ramp = column / max(H - 1, 1)
    row_scale = 10.0 ** jax.random.uniform(row_key, (TOKENS, 1), jnp.float32)
    base = jax.random.truncated_normal(base_key, -4.0, 4.0, (TOKENS, H * DV), jnp.float32)
    head_scale = 3.0 ** ramp
    return (base * head_scale[None, :] * row_scale).astype(jnp.bfloat16)


def with_ends(array, stream_key, least, largest):
    dims = array.shape
    spot = [jax.random.randint(jax.random.fold_in(stream_key, axis), (), 0, dims[axis]) for axis in range(len(dims))]
    array = array.at[tuple(spot)].set(least)
    longest = dims.index(max(dims))
    spot[longest] = (spot[longest] + 1) % dims[longest]
    return array.at[tuple(spot)].set(largest)


def block_scale(stream_key, dims, cuts, low, top_value):
    def one(position, blocks):
        draws = jax.random.uniform(jax.random.fold_in(jax.random.fold_in(stream_key, 6), position), (blocks,), jnp.float32, low / len(cuts), top_value / len(cuts))
        return jnp.repeat(jnp.exp(draws), dims[position] // blocks).reshape((-1,) + (1,) * (len(dims) - position - 1))

    gain = one(*cuts[0])
    for cut in cuts[1:]:
        gain = gain * one(*cut)
    return gain


def normal_values(own_key, dims, scale, most, pieces=(), held_as=jnp.bfloat16):
    values = scale * jax.random.normal(own_key, dims, jnp.float32)
    if pieces:
        values = values * block_scale(own_key, dims, pieces, -0.22, 0.18)
    return jnp.clip(values, -most, most).astype(held_as)


def setup_inputs(seed: int = 0) -> dict:
    key_list = jax.random.split(jax.random.key(seed), 6)
    queries = normal_values(key_list[0], (TOKENS, H * DK), 1.0, 6.0, ((0, 32), (1, 8)))
    keys = normal_values(key_list[1], (TOKENS, H * DK), DK ** -0.5, 0.5, ((0, 32), (1, 8)))
    values = draw_values(jax.random.fold_in(key_list[5], 71), 0)
    norm_gain = jnp.clip(1.0 + 0.18 * jax.random.normal(key_list[3], (H * DV,), jnp.float32), 0.099609375, 1.8984375).astype(jnp.bfloat16)
    level_index = with_ends(jax.random.randint(key_list[4], (LEV, H, TOKENS), 1, 257), jax.random.fold_in(key_list[4], 1), 1, 256).astype(jnp.int32)
    return dict(queries=queries, keys=keys, values=values, norm_gain=norm_gain, level_index=level_index)


def one_head(packed):
    query_rows, key_rows, value_rows, weight_rows = packed
    stretches_all = TOKENS // STRETCH
    query_blocks = query_rows.reshape(stretches_all, STRETCH, DK).astype(jnp.float32)
    key_blocks = key_rows.reshape(stretches_all, STRETCH, DK).astype(jnp.float32)
    value_blocks = value_rows.reshape(stretches_all, STRETCH, DV).astype(jnp.float32)
    scores = jnp.einsum('cid,cjd->cij', query_blocks, key_blocks)
    causal = jnp.arange(STRETCH)[:, None] >= jnp.arange(STRETCH)[None, :]
    scores_low = jnp.where(causal, scores, 0.0).astype(jnp.bfloat16)
    intra = jnp.einsum('cij,cje->cie', scores_low.astype(jnp.float32), value_blocks).reshape(TOKENS, DV)
    mixed = intra * (weight_rows[0] * float(STRETCH) ** (-0.5))[:, None]
    block_sums = jnp.einsum('cjd,cje->cde', key_blocks, value_blocks)
    query_flat = query_rows.astype(jnp.float32)
    for bit_pos in range(STRETCH_BITS + CTX_BITS):
        groups = stretches_all >> bit_pos + 1
        width_rows = 2 ** bit_pos * STRETCH
        paired = block_sums.reshape(groups, 2, DK, DV)
        lower_half = paired[:, 0].astype(jnp.bfloat16).astype(jnp.float32)
        upper_rows = query_flat.reshape(groups, 2, width_rows, DK)[:, 1]
        factor = (weight_rows[1 + bit_pos] * float(width_rows) ** (-0.5)).reshape(groups, 2, width_rows)[:, 1]
        level_term = jnp.einsum('gtd,gde->gte', upper_rows, lower_half) * factor[:, :, None]
        mixed = mixed.reshape(groups, 2, width_rows, DV).at[:, 1].add(level_term).reshape(TOKENS, DV)
        block_sums = lax.optimization_barrier(jnp.sum(paired, axis=1))
    return mixed

def reference(queries, keys, values, norm_gain, level_index):
    packed = (queries.reshape(TOKENS, H, DK).transpose(1, 0, 2), keys.reshape(TOKENS, H, DK).transpose(1, 0, 2), values.reshape(TOKENS, H, DV).transpose(1, 0, 2), level_index.astype(jnp.float32).transpose(1, 0, 2) / 256.0)
    mixed = lax.map(one_head, packed)
    flat = mixed.transpose(1, 0, 2).reshape(TOKENS, H * DV)
    square_sum = lax.optimization_barrier(jnp.sum(flat * flat, axis=1))
    inv_rms = lax.rsqrt(square_sum / (H * DV) + 1e-06)
    return (flat * inv_rms[:, None] * norm_gain.astype(jnp.float32)).astype(jnp.bfloat16)
```

```python
import functools

import jax
import jax.numpy as jnp
from jax import lax
from jax.experimental import pallas as pl
from jax.experimental.pallas import tpu as pltpu
from jax.sharding import PartitionSpec as P

H = 32
DK = 128
DV = 64
STRETCH = 64
HEADS = 4
TOK = 1024
BLK = 256
Z = 8
VMEM_LIMIT = 32 * 1024 * 1024

NT = (((1,), (1,)), ((), ()))
NN = (((1,), (0,)), ((), ()))


def dot(a, b, dims):
    return lax.dot_general(a, b, dims, preferred_element_type=jnp.float32)


def weight_scale(level):
    span = STRETCH if level == 0 else STRETCH * 2 ** (level - 1)
    return float(span) ** (-0.5) / 256.0


def weight_row(li_ref, level, head, start, size):
    row = li_ref[level, head : head + 1, start : start + size]
    return row.astype(jnp.float32) * weight_scale(level)


def summary_kernel(k_ref, v_ref, s_ref):
    vt = v_ref[...].T
    for h in range(HEADS):
        s_ref[h * DV : (h + 1) * DV, :] = dot(
            vt[h * DV : (h + 1) * DV, :], k_ref[:, h * DK : (h + 1) * DK], NN
        )


def local_kernel(first_head, heads, q_ref, k_ref, v_ref, li_ref, m_ref):
    lane = lax.broadcasted_iota(jnp.int32, (1, BLK), 1)
    t_stretch = lane // STRETCH
    row = lax.broadcasted_iota(jnp.int32, (BLK, BLK), 0)
    col = lax.broadcasted_iota(jnp.int32, (BLK, BLK), 1)
    causal = (row // STRETCH == col // STRETCH) & (row <= col)
    zero = jnp.zeros((), jnp.bfloat16)
    vt_all = v_ref[...].T
    for h in range(heads):
        wh = first_head + h
        before = None
        first_half = None
        for b in range(TOK // BLK):
            r0 = b * BLK
            q = q_ref[r0 : r0 + BLK, h * DK : (h + 1) * DK]
            k = k_ref[r0 : r0 + BLK, h * DK : (h + 1) * DK]
            vt = vt_all[h * DV : (h + 1) * DV, r0 : r0 + BLK]
            sums = dot(
                jnp.concatenate(
                    [
                        jnp.where(t_stretch == 0, vt, zero),
                        jnp.where(t_stretch == 2, vt, zero),
                        jnp.where(t_stretch < 2, vt, zero),
                        vt,
                    ],
                    axis=0,
                ),
                k,
                NN,
            )
            total = sums[3 * DV :]
            rows = [k, sums[: 3 * DV].astype(jnp.bfloat16)]
            if b % 2 == 1:
                rows.append(before.astype(jnp.bfloat16))
            if b >= 2:
                rows.append(first_half.astype(jnp.bfloat16))
            prod = dot(jnp.concatenate(rows, axis=0), q, NT)
            low = jnp.where(causal, prod[:BLK], 0.0).astype(jnp.bfloat16)
            mix = dot(vt, low, NN) * weight_row(li_ref, 0, wh, r0, BLK)
            part = [prod[BLK + i * DV : BLK + (i + 1) * DV] for i in range(len(rows) + 1)]
            near = jnp.where(
                t_stretch == 1, part[0], jnp.where(t_stretch == 3, part[1], 0.0)
            )
            mix = mix + near * weight_row(li_ref, 1, wh, r0, BLK)
            mix = mix + jnp.where(t_stretch >= 2, part[2], 0.0) * weight_row(
                li_ref, 2, wh, r0, BLK
            )
            at = 3
            if b % 2 == 1:
                mix = mix + part[at] * weight_row(li_ref, 3, wh, r0, BLK)
                at += 1
            if b >= 2:
                mix = mix + part[at] * weight_row(li_ref, 4, wh, r0, BLK)
            m_ref[h * DV : (h + 1) * DV, r0 : r0 + BLK] = mix
            if b == 1:
                first_half = before + total
            before = total


def far_mix(h, rank, bits, states, q_ref, li_ref):
    rows = jnp.concatenate(
        [s[h * DV : (h + 1) * DV, :].astype(jnp.bfloat16) for s in states], axis=0
    )
    prod = dot(rows, q_ref[:, h * DK : (h + 1) * DK], NT)
    mix = None
    for i, bit in enumerate(bits):
        has = (rank >> bit) & 1
        w = jnp.where(has == 1, weight_row(li_ref, 5 + bit, h, 0, TOK), 0.0)
        term = prod[i * DV : (i + 1) * DV] * w
        mix = term if mix is None else mix + term
    return mix


def far_kernel(bits, q_ref, li_ref, *refs):
    state_refs, m_in, m_ref = refs[: len(bits)], refs[len(bits) : -1], refs[-1]
    rank = lax.axis_index("ctx")
    states = [r[...] for r in state_refs]
    per = HEADS // len(m_in)
    for h in range(HEADS):
        at = (h % per) * DV
        mix = far_mix(h, rank, bits, states, q_ref, li_ref)
        m_ref[h * DV : (h + 1) * DV, :] = m_in[h // per][at : at + DV, :] + mix


def last_kernel(q_ref, li_ref, l2_ref, a_ref, b_ref, c_ref, m_in, m_ref, ss_ref):
    rank = lax.axis_index("ctx")
    both = rank // Z == 3
    l4 = b_ref[...] + jnp.where(both, c_ref[...], a_ref[...])
    states = [l2_ref[...], a_ref[...], l4]
    squares = None
    for h in range(HEADS):
        mix = m_in[h * DV : (h + 1) * DV, :] + far_mix(
            h, rank, (2, 3, 4), states, q_ref, li_ref
        )
        m_ref[h * DV : (h + 1) * DV, :] = mix
        sq = jnp.sum(mix * mix, axis=0, keepdims=True)
        squares = sq if squares is None else squares + sq
    for i in range(TOK // 128):
        ss_ref[i : i + 1, :] = squares[:, i * 128 : (i + 1) * 128]


def norm_kernel(m_ref, g_ref, s0, s1, s2, s3, out_ref):
    total = (s0[...] + s1[...]) + (s2[...] + s3[...])
    inv = lax.rsqrt(total / (H * DV) + 1e-06)
    gain = g_ref[...].astype(jnp.float32)
    for i in range(TOK // 128):
        x = m_ref[:, i * 128 : (i + 1) * 128] * inv[i : i + 1, :]
        out_ref[i * 128 : (i + 1) * 128, :] = (x.T * gain).astype(jnp.bfloat16)


def call(kernel, outs, n_in, flops=0, moved=0, in_specs=None, name=None):
    whole = pl.BlockSpec(memory_space=pltpu.VMEM)
    return pl.pallas_call(
        kernel,
        out_shape=outs,
        in_specs=in_specs or [whole] * n_in,
        out_specs=jax.tree.map(lambda _: whole, outs),
        compiler_params=pltpu.CompilerParams(vmem_limit_bytes=VMEM_LIMIT),
        cost_estimate=pl.CostEstimate(flops=flops, bytes_accessed=moved, transcendentals=0),
        name=name,
    )


def f32(*shape):
    return jax.ShapeDtypeStruct(shape, jnp.float32)


def on_device(queries, keys, values, norm_gain, level_index):
    ctx = lax.axis_size("ctx")
    ys = ctx // Z
    state = f32(HEADS * DV, DK)
    mixed = f32(HEADS * DV, TOK)

    def over_ctx(x, move):
        pairs = [(r, move(r // Z, r % Z)) for r in range(ctx)]
        return lax.ppermute(x, "ctx", [(r, y * Z + z) for r, (y, z) in pairs if y < ys])

    own = call(summary_kernel, state, 2, 268_000_000, 1_700_000, name="summary")(keys, values)
    l0 = over_ctx(own, lambda y, z: (y, z ^ 1))
    pair = own + l0
    l1 = over_ctx(pair, lambda y, z: (y, z ^ 2))
    quad = pair + l1
    hop = (6, 7, 4, 5, 2, 3, 0, 1)
    l2 = over_ctx(quad, lambda y, z: (y, hop[z]))
    group = quad + l2
    up1 = over_ctx(group, lambda y, z: (y + 1, z))
    up2 = over_ctx(group, lambda y, z: (y + 2, z))
    up3 = over_ctx(group, lambda y, z: (y + 3, z))

    half = HEADS // 2
    parts = []
    for p in range(2):
        specs = [
            pl.BlockSpec((TOK, half * DK), lambda i, p=p: (0, p)),
            pl.BlockSpec((TOK, half * DK), lambda i, p=p: (0, p)),
            pl.BlockSpec((TOK, half * DV), lambda i, p=p: (0, p)),
            pl.BlockSpec(level_index.shape, lambda i: (0, 0, 0)),
        ]
        parts.append(
            pl.pallas_call(
                functools.partial(local_kernel, p * half, half),
                grid=(1,),
                out_shape=f32(half * DV, TOK),
                in_specs=specs,
                out_specs=pl.BlockSpec((half * DV, TOK), lambda i: (0, 0)),
                compiler_params=pltpu.CompilerParams(vmem_limit_bytes=VMEM_LIMIT),
                cost_estimate=pl.CostEstimate(
                    flops=1_000_000_000, bytes_accessed=2_000_000, transcendentals=0
                ),
                name="local%d" % p,
            )(queries, keys, values, level_index)
        )
    near = call(
        functools.partial(far_kernel, (0, 1)), mixed, 6, 134_000_000, 3_000_000, name="far01"
    )(queries, level_index, l0, l1, *parts)
    flat, squares = call(
        last_kernel, (mixed, f32(8, 128)), 7, 200_000_000, 3_000_000, name="last"
    )(queries, level_index, l2, up1, up2, up3, near)

    squares = squares + lax.ppermute(squares, "head", [(i, i ^ 1) for i in range(8)])
    others = [
        lax.ppermute(squares, "head", [(i, (i + 2 * n) % 8) for i in range(8)]) for n in (1, 3, 2)
    ]
    return call(
        norm_kernel,
        jax.ShapeDtypeStruct((TOK, HEADS * DV), jnp.bfloat16),
        6,
        1_000_000,
        1_500_000,
        name="norm",
    )(flat, norm_gain.reshape(1, HEADS * DV), squares, *others)


def solution(mesh):
    in_specs = (
        P("ctx", "head"),
        P("ctx", "head"),
        P("ctx", "head"),
        P("head"),
        P(None, "head", "ctx"),
    )
    out_specs = P("ctx", "head")
    return jax.shard_map(
        on_device, mesh=mesh, in_specs=in_specs, out_specs=out_specs, check_vma=False
    )
```

```python
import functools

import jax
import jax.numpy as jnp
from jax import lax
from jax.experimental import pallas as pl
from jax.experimental.pallas import tpu as pltpu
from jax.sharding import PartitionSpec as P

H = 32
DK = 128
DV = 64
STRETCH = 64
HEADS = 4
TOK = 1024
BLK = 256
Z = 8
VMEM_LIMIT = 32 * 1024 * 1024
CHUNKS = 1
PER = HEADS // CHUNKS

NT = (((1,), (1,)), ((), ()))
NN = (((1,), (0,)), ((), ()))


def dot(a, b, dims):
    return lax.dot_general(a, b, dims, preferred_element_type=jnp.float32)


def weight_scale(level):
    span = STRETCH if level == 0 else STRETCH * 2 ** (level - 1)
    return float(span) ** (-0.5) / 256.0


def weight_row(li_ref, level, head, start, size):
    row = li_ref[level, head : head + 1, start : start + size]
    return row.astype(jnp.float32) * weight_scale(level)


def summary_kernel(k_hbm, v_hbm, *refs):
    outs, (k_ref, vt_ref, v_ref, sems) = refs[:CHUNKS], refs[CHUNKS:]
    copies = []
    for b in range(TOK // BLK):
        rows = pl.ds(b * BLK, BLK)
        pair = (
            pltpu.make_async_copy(v_hbm.at[rows], v_ref.at[rows], sems.at[0, b]),
            pltpu.make_async_copy(k_hbm.at[rows], k_ref.at[rows], sems.at[1, b]),
        )
        for copy in pair:
            copy.start()
        copies.append(pair)
    totals = [None] * HEADS
    for b in range(TOK // BLK):
        for copy in copies[b]:
            copy.wait()
        r0 = b * BLK
        vt = v_ref[r0 : r0 + BLK, :].T
        vt_ref[:, r0 : r0 + BLK] = vt
        for h in range(HEADS):
            part = dot(
                vt[h * DV : (h + 1) * DV, :], k_ref[r0 : r0 + BLK, h * DK : (h + 1) * DK], NN
            )
            totals[h] = part if b == 0 else totals[h] + part
    for h in range(HEADS):
        at = (h % PER) * DV
        outs[h // PER][at : at + DV, :] = totals[h]


def local_kernel(first_head, heads, q_ref, k_ref, vt_ref, li_ref, m_ref):
    lane = lax.broadcasted_iota(jnp.int32, (1, BLK), 1)
    t_stretch = lane // STRETCH
    row = lax.broadcasted_iota(jnp.int32, (BLK, BLK), 0)
    col = lax.broadcasted_iota(jnp.int32, (BLK, BLK), 1)
    causal = (row // STRETCH == col // STRETCH) & (row <= col)
    zero = jnp.zeros((), jnp.bfloat16)
    for h in range(heads):
        wh = first_head + h
        before = None
        first_half = None
        for b in range(TOK // BLK):
            r0 = b * BLK
            q = q_ref[r0 : r0 + BLK, h * DK : (h + 1) * DK]
            k = k_ref[r0 : r0 + BLK, h * DK : (h + 1) * DK]
            vt = vt_ref[h * DV : (h + 1) * DV, r0 : r0 + BLK]
            sums = dot(
                jnp.concatenate(
                    [
                        jnp.where(t_stretch == 0, vt, zero),
                        jnp.where(t_stretch == 2, vt, zero),
                        jnp.where(t_stretch < 2, vt, zero),
                        vt,
                    ],
                    axis=0,
                ),
                k,
                NN,
            )
            total = sums[3 * DV :]
            rows = [k, sums[: 3 * DV].astype(jnp.bfloat16)]
            if b % 2 == 1:
                rows.append(before.astype(jnp.bfloat16))
            if b >= 2:
                rows.append(first_half.astype(jnp.bfloat16))
            prod = dot(jnp.concatenate(rows, axis=0), q, NT)
            low = jnp.where(causal, prod[:BLK], 0.0).astype(jnp.bfloat16)
            mix = dot(vt, low, NN) * weight_row(li_ref, 0, wh, r0, BLK)
            part = [prod[BLK + i * DV : BLK + (i + 1) * DV] for i in range(len(rows) + 1)]
            near = jnp.where(
                t_stretch == 1, part[0], jnp.where(t_stretch == 3, part[1], 0.0)
            )
            mix = mix + near * weight_row(li_ref, 1, wh, r0, BLK)
            mix = mix + jnp.where(t_stretch >= 2, part[2], 0.0) * weight_row(
                li_ref, 2, wh, r0, BLK
            )
            at = 3
            if b % 2 == 1:
                mix = mix + part[at] * weight_row(li_ref, 3, wh, r0, BLK)
                at += 1
            if b >= 2:
                mix = mix + part[at] * weight_row(li_ref, 4, wh, r0, BLK)
            m_ref[h * DV : (h + 1) * DV, r0 : r0 + BLK] = mix
            if b == 1:
                first_half = before + total
            before = total


def far_mix(h, rank, bits, states, q_ref, li_ref):
    at = (h % PER) * DV
    rows = jnp.concatenate(
        [s[h // PER][at : at + DV, :].astype(jnp.bfloat16) for s in states], axis=0
    )
    prod = dot(rows, q_ref[:, h * DK : (h + 1) * DK], NT)
    mix = None
    for i, bit in enumerate(bits):
        has = (rank >> bit) & 1
        w = jnp.where(has == 1, weight_row(li_ref, 5 + bit, h, 0, TOK), 0.0)
        term = prod[i * DV : (i + 1) * DV] * w
        mix = term if mix is None else mix + term
    return mix


def grouped(refs, n):
    return [refs[i * CHUNKS : (i + 1) * CHUNKS] for i in range(n)]


def far_kernel(bits, q_ref, li_ref, *refs):
    n = len(bits) * CHUNKS
    states, m_in, m_ref = grouped(refs[:n], len(bits)), refs[n:-1], refs[-1]
    rank = lax.axis_index("ctx")
    per = HEADS // len(m_in)
    for h in range(HEADS):
        at = (h % per) * DV
        mix = far_mix(h, rank, bits, states, q_ref, li_ref)
        m_ref[h * DV : (h + 1) * DV, :] = m_in[h // per][at : at + DV, :] + mix


def last_kernel(q_ref, li_ref, *refs):
    (m_in, m_ref, ss_ref) = refs[2 * CHUNKS :]
    states = [[refs[c][...] + refs[CHUNKS + c][...] for c in range(CHUNKS)]]
    rank = lax.axis_index("ctx")
    squares = None
    for h in range(HEADS):
        mix = m_in[h * DV : (h + 1) * DV, :] + far_mix(h, rank, (4,), states, q_ref, li_ref)
        m_ref[h * DV : (h + 1) * DV, :] = mix
        sq = jnp.sum(mix * mix, axis=0, keepdims=True)
        squares = sq if squares is None else squares + sq
    for i in range(TOK // 128):
        ss_ref[i : i + 1, :] = squares[:, i * 128 : (i + 1) * 128]


def turn_kernel(m_ref, g_ref, t_ref):
    gain = g_ref[...].astype(jnp.float32)
    for i in range(TOK // 128):
        t_ref[i * 128 : (i + 1) * 128, :] = m_ref[:, i * 128 : (i + 1) * 128].T * gain


def norm_kernel(t_ref, s0, s1, s2, s3, out_hbm, o_ref, sems):
    total = (s0[...] + s1[...]) + (s2[...] + s3[...])
    inv = lax.rsqrt(total / (H * DV) + 1e-06).T
    copies = []
    for i in range(TOK // 128):
        rows = slice(i * 128, (i + 1) * 128)
        o_ref[rows, :] = (t_ref[rows, :] * inv[:, i : i + 1]).astype(jnp.bfloat16)
        rows = pl.ds(i * 128, 128)
        copies.append(pltpu.make_async_copy(o_ref.at[rows], out_hbm.at[rows], sems.at[i]))
        copies[-1].start()
    for copy in copies:
        copy.wait()


WHOLE = pl.BlockSpec(memory_space=pltpu.VMEM)
HBM = pl.BlockSpec(memory_space=pltpu.HBM)


def call(
    kernel,
    outs,
    n_in,
    name,
    flops=0,
    moved=0,
    in_specs=None,
    out_specs=None,
    scratch=(),
    grid=(),
    vmem=VMEM_LIMIT,
):
    return pl.pallas_call(
        kernel,
        grid=grid,
        out_shape=outs,
        in_specs=in_specs or [WHOLE] * n_in,
        out_specs=out_specs or jax.tree.map(lambda _: WHOLE, outs),
        scratch_shapes=scratch,
        compiler_params=pltpu.CompilerParams(vmem_limit_bytes=vmem),
        cost_estimate=pl.CostEstimate(flops=flops, bytes_accessed=moved, transcendentals=0),
        name=name,
    )


def f32(*shape):
    return jax.ShapeDtypeStruct(shape, jnp.float32)


def in_hbm(x):
    return pltpu.with_memory_space_constraint(x, pltpu.HBM)


def bf16(*shape):
    return jax.ShapeDtypeStruct(shape, jnp.bfloat16)


def on_device(queries, keys, values, norm_gain, level_index):
    ctx = lax.axis_size("ctx")
    state = f32(PER * DV, DK)
    mixed = f32(HEADS * DV, TOK)

    def over_ctx(chunks, move):
        pairs = []
        for r in range(ctx):
            to = move(r // Z, r % Z)
            if to is not None:
                pairs.append((r, to[0] * Z + to[1]))
        return [lax.ppermute(x, "ctx", pairs) for x in chunks]

    def add(a, b):
        return [x + y for x, y in zip(a, b)]

    *own, keys_here, values_turned = call(
        summary_kernel,
        [state] * CHUNKS + [bf16(TOK, HEADS * DK), bf16(HEADS * DV, TOK)],
        2,
        "summary",
        268_000_000,
        3_200_000,
        in_specs=[HBM, HBM],
        scratch=[
            pltpu.VMEM((TOK, HEADS * DV), jnp.bfloat16),
            pltpu.SemaphoreType.DMA((2, TOK // BLK)),
        ],
    )(in_hbm(keys), in_hbm(values))

    half = HEADS // 2
    parts = []
    for p in range(2):
        specs = [
            pl.BlockSpec((TOK, half * DK), lambda i, p=p: (0, p)),
            pl.BlockSpec((TOK, half * DK), lambda i, p=p: (0, p)),
            pl.BlockSpec((half * DV, TOK), lambda i, p=p: (p, 0)),
            pl.BlockSpec(level_index.shape, lambda i: (0, 0, 0)),
        ]
        parts.append(
            call(
                functools.partial(local_kernel, p * half, half),
                f32(half * DV, TOK),
                4,
                "local%d" % p,
                1_000_000_000,
                2_000_000,
                in_specs=specs,
                out_specs=pl.BlockSpec((half * DV, TOK), lambda i: (0, 0)),
                grid=(1,),
            )(queries, keys_here, values_turned, level_index)
        )

    l0 = over_ctx(own, lambda y, z: (y, z ^ 1))
    l0[-1], parts[0] = lax.optimization_barrier((l0[-1], parts[0]))
    pair = add(own, l0)
    l1 = over_ctx(pair, lambda y, z: (y, z ^ 3))
    l1[-1], parts[1] = lax.optimization_barrier((l1[-1], parts[1]))
    quad = add(pair, l1)
    hop = (6, 7, 4, 5, 2, 3, 0, 1)
    l2 = over_ctx(quad, lambda y, z: (y, hop[z]))
    group = add(quad, l2)
    l3 = over_ctx(group, lambda y, z: (y ^ 1, z))
    up = [over_ctx(group, lambda y, z, k=k: (y ^ k, z)) for k in (3, 2)]
    near = call(
        functools.partial(far_kernel, (0, 1, 2, 3)),
        mixed,
        4 + 4 * CHUNKS,
        "far0123",
        268_000_000,
        3_000_000,
    )(queries, level_index, *l0, *l1, *l2, *l3, *parts)
    flat, squares = call(
        last_kernel, (mixed, f32(8, 128)), 3 + 2 * CHUNKS, "last", 67_000_000, 3_000_000
    )(queries, level_index, *up[0], *up[1], near)

    turned = call(turn_kernel, f32(TOK, HEADS * DV), 2, "turn", 1_000_000, 2_000_000)(
        flat, norm_gain.reshape(1, HEADS * DV)
    )
    def over_head(x, move):
        pairs = [(i, (i // 2, i % 2)) for i in range(8)]
        return lax.ppermute(
            x, "head", [(i, to[0] * 2 + to[1]) for i, to in ((i, move(*xc)) for i, xc in pairs)]
        )

    squares = squares + over_head(squares, lambda x, c: (x, 1 - c))
    one = over_head(squares, lambda x, c: (x ^ (1 if c == 0 else 3), c))
    two = over_head(squares, lambda x, c: (x ^ 2, c))
    three = over_head(one, lambda x, c: (x, 1 - c))
    others = (one, two, three)
    return call(
        norm_kernel,
        bf16(TOK, HEADS * DV),
        5,
        "norm",
        1_000_000,
        1_500_000,
        out_specs=HBM,
        scratch=[pltpu.VMEM((TOK, HEADS * DV), jnp.bfloat16), pltpu.SemaphoreType.DMA((8,))],
    )(turned, squares, *others)


def solution(mesh):
    in_specs = (
        P("ctx", "head"),
        P("ctx", "head"),
        P("ctx", "head"),
        P("head"),
        P(None, "head", "ctx"),
    )
    out_specs = P("ctx", "head")
    return jax.shard_map(
        on_device, mesh=mesh, in_specs=in_specs, out_specs=out_specs, check_vma=False
    )
```

```python
import functools

import jax
import jax.numpy as jnp
from jax import lax
from jax.experimental import pallas as pl
from jax.experimental.pallas import tpu as pltpu
from jax.sharding import PartitionSpec as P

H = 32
DK = 128
DV = 64
STRETCH = 64
HEADS = 4
TOK = 1024
BLK = 256
Z = 8
VMEM_LIMIT = 32 * 1024 * 1024
CHUNKS = 1
PER = HEADS // CHUNKS

NT = (((1,), (1,)), ((), ()))
NN = (((1,), (0,)), ((), ()))


def dot(a, b, dims):
    return lax.dot_general(a, b, dims, preferred_element_type=jnp.float32)


def weight_scale(level):
    span = STRETCH if level == 0 else STRETCH * 2 ** (level - 1)
    return float(span) ** (-0.5) / 256.0


def weight_row(li_ref, level, head, start, size):
    row = li_ref[level, head : head + 1, start : start + size]
    return row.astype(jnp.float32) * weight_scale(level)


def summary_kernel(k_hbm, v_hbm, *refs):
    outs, (k_ref, vt_ref, v_ref, sems) = refs[:CHUNKS], refs[CHUNKS:]
    copies = []
    for b in range(TOK // BLK):
        rows = pl.ds(b * BLK, BLK)
        pair = (
            pltpu.make_async_copy(v_hbm.at[rows], v_ref.at[rows], sems.at[0, b]),
            pltpu.make_async_copy(k_hbm.at[rows], k_ref.at[rows], sems.at[1, b]),
        )
        for copy in pair:
            copy.start()
        copies.append(pair)
    totals = [None] * HEADS
    for b in range(TOK // BLK):
        for copy in copies[b]:
            copy.wait()
        r0 = b * BLK
        vt = v_ref[r0 : r0 + BLK, :].T
        vt_ref[:, r0 : r0 + BLK] = vt
        for h in range(HEADS):
            part = dot(
                vt[h * DV : (h + 1) * DV, :], k_ref[r0 : r0 + BLK, h * DK : (h + 1) * DK], NN
            )
            totals[h] = part if b == 0 else totals[h] + part
    for h in range(HEADS):
        at = (h % PER) * DV
        outs[h // PER][at : at + DV, :] = totals[h]


def local_kernel(first_head, heads, q_ref, k_ref, vt_ref, li_ref, m_ref):
    lane = lax.broadcasted_iota(jnp.int32, (1, BLK), 1)
    t_stretch = lane // STRETCH
    row = lax.broadcasted_iota(jnp.int32, (BLK, BLK), 0)
    col = lax.broadcasted_iota(jnp.int32, (BLK, BLK), 1)
    causal = (row // STRETCH == col // STRETCH) & (row <= col)
    zero = jnp.zeros((), jnp.bfloat16)
    before = [None] * heads
    first_half = [None] * heads
    for b in range(TOK // BLK):
        r0 = b * BLK
        for h in range(heads):
            wh = first_head + h
            q = q_ref[r0 : r0 + BLK, h * DK : (h + 1) * DK]
            k = k_ref[r0 : r0 + BLK, h * DK : (h + 1) * DK]
            vt = vt_ref[h * DV : (h + 1) * DV, r0 : r0 + BLK]
            sums = dot(
                jnp.concatenate(
                    [
                        jnp.where(t_stretch == 0, vt, zero),
                        jnp.where(t_stretch == 2, vt, zero),
                        jnp.where(t_stretch < 2, vt, zero),
                        vt,
                    ],
                    axis=0,
                ),
                k,
                NN,
            )
            total = sums[3 * DV :]
            rows = [k, sums[: 3 * DV].astype(jnp.bfloat16)]
            if b % 2 == 1:
                rows.append(before[h].astype(jnp.bfloat16))
            if b >= 2:
                rows.append(first_half[h].astype(jnp.bfloat16))
            prod = dot(jnp.concatenate(rows, axis=0), q, NT)
            low = jnp.where(causal, prod[:BLK], 0.0).astype(jnp.bfloat16)
            mix = dot(vt, low, NN) * weight_row(li_ref, 0, wh, r0, BLK)
            part = [prod[BLK + i * DV : BLK + (i + 1) * DV] for i in range(len(rows) + 1)]
            near = jnp.where(
                t_stretch == 1, part[0], jnp.where(t_stretch == 3, part[1], 0.0)
            )
            mix = mix + near * weight_row(li_ref, 1, wh, r0, BLK)
            mix = mix + jnp.where(t_stretch >= 2, part[2], 0.0) * weight_row(
                li_ref, 2, wh, r0, BLK
            )
            at = 3
            if b % 2 == 1:
                mix = mix + part[at] * weight_row(li_ref, 3, wh, r0, BLK)
                at += 1
            if b >= 2:
                mix = mix + part[at] * weight_row(li_ref, 4, wh, r0, BLK)
            m_ref[h * DV : (h + 1) * DV, r0 : r0 + BLK] = mix
            if b == 1:
                first_half[h] = before[h] + total
            before[h] = total


def far_mix(h, rank, bits, states, q_ref, li_ref):
    at = (h % PER) * DV
    rows = jnp.concatenate(
        [s[h // PER][at : at + DV, :].astype(jnp.bfloat16) for s in states], axis=0
    )
    prod = dot(rows, q_ref[:, h * DK : (h + 1) * DK], NT)
    mix = None
    for i, bit in enumerate(bits):
        has = (rank >> bit) & 1
        w = jnp.where(has == 1, weight_row(li_ref, 5 + bit, h, 0, TOK), 0.0)
        term = prod[i * DV : (i + 1) * DV] * w
        mix = term if mix is None else mix + term
    return mix


def grouped(refs, n):
    return [refs[i * CHUNKS : (i + 1) * CHUNKS] for i in range(n)]


def far_kernel(bits, q_ref, li_ref, *refs):
    n = len(bits) * CHUNKS
    states, m_in, m_ref = grouped(refs[:n], len(bits)), refs[n:-1], refs[-1]
    rank = lax.axis_index("ctx")
    per = HEADS // len(m_in)
    for h in range(HEADS):
        at = (h % per) * DV
        mix = far_mix(h, rank, bits, states, q_ref, li_ref)
        m_ref[h * DV : (h + 1) * DV, :] = m_in[h // per][at : at + DV, :] + mix


def last_kernel(q_ref, li_ref, *refs):
    l3, up3, up2 = grouped(refs[: 3 * CHUNKS], 3)
    m_in, m_ref, ss_ref = refs[3 * CHUNKS :]
    states = [l3, [a[...] + b[...] for a, b in zip(up3, up2)]]
    rank = lax.axis_index("ctx")
    squares = None
    for h in range(HEADS):
        mix = m_in[h * DV : (h + 1) * DV, :] + far_mix(h, rank, (3, 4), states, q_ref, li_ref)
        m_ref[h * DV : (h + 1) * DV, :] = mix
        sq = jnp.sum(mix * mix, axis=0, keepdims=True)
        squares = sq if squares is None else squares + sq
    for i in range(TOK // 128):
        ss_ref[i : i + 1, :] = squares[:, i * 128 : (i + 1) * 128]


def gain_kernel(m_ref, g_ref, t_ref):
    t_ref[...] = m_ref[...] * g_ref[...].astype(jnp.float32).T


def norm_kernel(m_ref, s0, s1, s2, s3, out_hbm, o_ref, sems):
    total = (s0[...] + s1[...]) + (s2[...] + s3[...])
    inv = lax.rsqrt(total / (H * DV) + 1e-06)
    copies = []
    for i in range(TOK // 128):
        x = (m_ref[:, i * 128 : (i + 1) * 128] * inv[i : i + 1, :]).astype(jnp.bfloat16)
        o_ref[i * 128 : (i + 1) * 128, :] = x.T
        rows = pl.ds(i * 128, 128)
        copies.append(pltpu.make_async_copy(o_ref.at[rows], out_hbm.at[rows], sems.at[i]))
        copies[-1].start()
    for copy in copies:
        copy.wait()


WHOLE = pl.BlockSpec(memory_space=pltpu.VMEM)
HBM = pl.BlockSpec(memory_space=pltpu.HBM)


def call(
    kernel,
    outs,
    n_in,
    name,
    flops=0,
    moved=0,
    in_specs=None,
    out_specs=None,
    scratch=(),
    grid=(),
    vmem=VMEM_LIMIT,
):
    return pl.pallas_call(
        kernel,
        grid=grid,
        out_shape=outs,
        in_specs=in_specs or [WHOLE] * n_in,
        out_specs=out_specs or jax.tree.map(lambda _: WHOLE, outs),
        scratch_shapes=scratch,
        compiler_params=pltpu.CompilerParams(vmem_limit_bytes=vmem),
        cost_estimate=pl.CostEstimate(flops=flops, bytes_accessed=moved, transcendentals=0),
        name=name,
    )


def f32(*shape):
    return jax.ShapeDtypeStruct(shape, jnp.float32)


def in_hbm(x):
    return pltpu.with_memory_space_constraint(x, pltpu.HBM)


def bf16(*shape):
    return jax.ShapeDtypeStruct(shape, jnp.bfloat16)


def on_device(queries, keys, values, norm_gain, level_index):
    ctx = lax.axis_size("ctx")
    state = f32(PER * DV, DK)
    mixed = f32(HEADS * DV, TOK)

    def over_ctx(chunks, move):
        pairs = []
        for r in range(ctx):
            to = move(r // Z, r % Z)
            if to is not None:
                pairs.append((r, to[0] * Z + to[1]))
        return [lax.ppermute(x, "ctx", pairs) for x in chunks]

    def add(a, b):
        return [x + y for x, y in zip(a, b)]

    *own, keys_here, values_turned = call(
        summary_kernel,
        [state] * CHUNKS + [bf16(TOK, HEADS * DK), bf16(HEADS * DV, TOK)],
        2,
        "summary",
        268_000_000,
        3_200_000,
        in_specs=[HBM, HBM],
        scratch=[
            pltpu.VMEM((TOK, HEADS * DV), jnp.bfloat16),
            pltpu.SemaphoreType.DMA((2, TOK // BLK)),
        ],
    )(in_hbm(keys), in_hbm(values))

    half = HEADS // 2
    parts = []
    for p in range(2):
        parts.append(
            call(
                functools.partial(local_kernel, p * half, half),
                f32(half * DV, TOK),
                4,
                "local%d" % p,
                1_000_000_000,
                2_000_000,
                in_specs=[
                    pl.BlockSpec((TOK, half * DK), lambda i, p=p: (0, p)),
                    pl.BlockSpec((TOK, half * DK), lambda i, p=p: (0, p)),
                    pl.BlockSpec((half * DV, TOK), lambda i, p=p: (p, 0)),
                    pl.BlockSpec(level_index.shape, lambda i: (0, 0, 0)),
                ],
                out_specs=pl.BlockSpec((half * DV, TOK), lambda i: (0, 0)),
                grid=(1,),
            )(queries, keys_here, values_turned, level_index)
        )

    l0 = over_ctx(own, lambda y, z: (y, z ^ 1))
    l0[-1], parts[0] = lax.optimization_barrier((l0[-1], parts[0]))
    pair = add(own, l0)
    l1 = over_ctx(pair, lambda y, z: (y, z ^ 3))
    l1[-1], parts[1] = lax.optimization_barrier((l1[-1], parts[1]))
    quad = add(pair, l1)
    hop = (7, 6, 5, 4, 3, 2, 1, 0)
    l2 = over_ctx(quad, lambda y, z: (y, hop[z]))
    group = add(quad, l2)
    l3 = over_ctx(group, lambda y, z: (y ^ 1, z))
    up = [over_ctx(group, lambda y, z, k=k: (y ^ k, z)) for k in (3, 2)]
    near = call(
        functools.partial(far_kernel, (0, 1, 2)),
        mixed,
        4 + 3 * CHUNKS,
        "far012",
        268_000_000,
        3_000_000,
    )(queries, level_index, *l0, *l1, *l2, *parts)
    flat, squares = call(
        last_kernel, (mixed, f32(8, 128)), 3 + 3 * CHUNKS, "last", 67_000_000, 3_000_000
    )(queries, level_index, *l3, *up[0], *up[1], near)

    scaled = call(gain_kernel, mixed, 2, "gain", 1_000_000, 2_000_000)(
        flat, norm_gain.reshape(1, HEADS * DV)
    )
    def over_head(x, move):
        pairs = [(i, (i // 2, i % 2)) for i in range(8)]
        return lax.ppermute(
            x, "head", [(i, to[0] * 2 + to[1]) for i, to in ((i, move(*xc)) for i, xc in pairs)]
        )

    squares = squares + over_head(squares, lambda x, c: (x, 1 - c))
    others = [over_head(squares, lambda x, c, k=k: (x ^ k, 1 - c)) for k in (1, 3, 2)]
    return call(
        norm_kernel,
        bf16(TOK, HEADS * DV),
        5,
        "norm",
        1_000_000,
        1_500_000,
        out_specs=HBM,
        scratch=[pltpu.VMEM((TOK, HEADS * DV), jnp.bfloat16), pltpu.SemaphoreType.DMA((8,))],
    )(scaled, squares, *others)


def solution(mesh):
    in_specs = (
        P("ctx", "head"),
        P("ctx", "head"),
        P("ctx", "head"),
        P("head"),
        P(None, "head", "ctx"),
    )
    out_specs = P("ctx", "head")
    return jax.shard_map(
        on_device, mesh=mesh, in_specs=in_specs, out_specs=out_specs, check_vma=False
    )
```

```python
import functools

import jax
import jax.numpy as jnp
from jax import lax
from jax.experimental import pallas as pl
from jax.experimental.pallas import tpu as pltpu
from jax.sharding import PartitionSpec as P

H = 32
DK = 128
DV = 64
STRETCH = 64
HEADS = 4
TOK = 1024
BLK = 256
SUM_BLK = 512
Z = 8
VMEM_LIMIT = 32 * 1024 * 1024
CHUNKS = 1
PER = HEADS // CHUNKS

NT = (((1,), (1,)), ((), ()))
NN = (((1,), (0,)), ((), ()))


def dot(a, b, dims):
    return lax.dot_general(a, b, dims, preferred_element_type=jnp.float32)


def weight_scale(level):
    span = STRETCH if level == 0 else STRETCH * 2 ** (level - 1)
    return float(span) ** (-0.5) / 256.0


def weight_row(li_ref, level, head, start, size):
    row = li_ref[level, head : head + 1, start : start + size]
    return row.astype(jnp.float32) * weight_scale(level)


def summary_kernel(k_hbm, v_hbm, *refs):
    outs, (k_ref, vt_ref, v_ref, sems) = refs[:CHUNKS], refs[CHUNKS:]
    copies = []
    for b in range(TOK // SUM_BLK):
        rows = pl.ds(b * SUM_BLK, SUM_BLK)
        pair = (
            pltpu.make_async_copy(v_hbm.at[rows], v_ref.at[rows], sems.at[0, b]),
            pltpu.make_async_copy(k_hbm.at[rows], k_ref.at[rows], sems.at[1, b]),
        )
        for copy in pair:
            copy.start()
        copies.append(pair)
    totals = [None] * HEADS
    for b in range(TOK // SUM_BLK):
        for copy in copies[b]:
            copy.wait()
        r0 = b * SUM_BLK
        vt = v_ref[r0 : r0 + SUM_BLK, :].T
        vt_ref[:, r0 : r0 + SUM_BLK] = vt
        for h in range(HEADS):
            part = dot(
                vt[h * DV : (h + 1) * DV, :], k_ref[r0 : r0 + SUM_BLK, h * DK : (h + 1) * DK], NN
            )
            totals[h] = part if b == 0 else totals[h] + part
    for h in range(HEADS):
        at = (h % PER) * DV
        outs[h // PER][at : at + DV, :] = totals[h]


def local_kernel(first_head, heads, q_ref, k_ref, vt_ref, li_ref, m_ref):
    lane = lax.broadcasted_iota(jnp.int32, (1, BLK), 1)
    t_stretch = lane // STRETCH
    row = lax.broadcasted_iota(jnp.int32, (BLK, BLK), 0)
    col = lax.broadcasted_iota(jnp.int32, (BLK, BLK), 1)
    causal = (row // STRETCH == col // STRETCH) & (row <= col)
    zero = jnp.zeros((), jnp.bfloat16)
    before = [None] * heads
    first_half = [None] * heads
    for b in range(TOK // BLK):
        r0 = b * BLK
        for h in range(heads):
            wh = first_head + h
            q = q_ref[r0 : r0 + BLK, h * DK : (h + 1) * DK]
            k = k_ref[r0 : r0 + BLK, h * DK : (h + 1) * DK]
            vt = vt_ref[h * DV : (h + 1) * DV, r0 : r0 + BLK]
            sums = dot(
                jnp.concatenate(
                    [
                        jnp.where(t_stretch == 0, vt, zero),
                        jnp.where(t_stretch == 2, vt, zero),
                        jnp.where(t_stretch < 2, vt, zero),
                        vt,
                    ],
                    axis=0,
                ),
                k,
                NN,
            )
            total = sums[3 * DV :]
            rows = [k, sums[: 3 * DV].astype(jnp.bfloat16)]
            if b % 2 == 1:
                rows.append(before[h].astype(jnp.bfloat16))
            if b >= 2:
                rows.append(first_half[h].astype(jnp.bfloat16))
            prod = dot(jnp.concatenate(rows, axis=0), q, NT)
            low = jnp.where(causal, prod[:BLK], 0.0).astype(jnp.bfloat16)
            mix = dot(vt, low, NN) * weight_row(li_ref, 0, wh, r0, BLK)
            part = [prod[BLK + i * DV : BLK + (i + 1) * DV] for i in range(len(rows) + 1)]
            near = jnp.where(
                t_stretch == 1, part[0], jnp.where(t_stretch == 3, part[1], 0.0)
            )
            mix = mix + near * weight_row(li_ref, 1, wh, r0, BLK)
            mix = mix + jnp.where(t_stretch >= 2, part[2], 0.0) * weight_row(
                li_ref, 2, wh, r0, BLK
            )
            at = 3
            if b % 2 == 1:
                mix = mix + part[at] * weight_row(li_ref, 3, wh, r0, BLK)
                at += 1
            if b >= 2:
                mix = mix + part[at] * weight_row(li_ref, 4, wh, r0, BLK)
            m_ref[h * DV : (h + 1) * DV, r0 : r0 + BLK] = mix
            if b == 1:
                first_half[h] = before[h] + total
            before[h] = total


def far_mix(h, rank, bits, states, q_ref, li_ref):
    at = (h % PER) * DV
    rows = jnp.concatenate(
        [s[h // PER][at : at + DV, :].astype(jnp.bfloat16) for s in states], axis=0
    )
    prod = dot(rows, q_ref[:, h * DK : (h + 1) * DK], NT)
    mix = None
    for i, bit in enumerate(bits):
        has = (rank >> bit) & 1
        w = jnp.where(has == 1, weight_row(li_ref, 5 + bit, h, 0, TOK), 0.0)
        term = prod[i * DV : (i + 1) * DV] * w
        mix = term if mix is None else mix + term
    return mix


def grouped(refs, n):
    return [refs[i * CHUNKS : (i + 1) * CHUNKS] for i in range(n)]


def far_kernel(bits, q_ref, li_ref, *refs):
    n = len(bits) * CHUNKS
    states, m_in, m_ref = grouped(refs[:n], len(bits)), refs[n:-1], refs[-1]
    rank = lax.axis_index("ctx")
    per = HEADS // len(m_in)
    for h in range(HEADS):
        at = (h % per) * DV
        mix = far_mix(h, rank, bits, states, q_ref, li_ref)
        m_ref[h * DV : (h + 1) * DV, :] = m_in[h // per][at : at + DV, :] + mix


def last_kernel(q_ref, li_ref, *refs):
    l3, up3, up2 = grouped(refs[: 3 * CHUNKS], 3)
    m_in, m_ref, ss_ref = refs[3 * CHUNKS :]
    states = [l3, [a[...] + b[...] for a, b in zip(up3, up2)]]
    rank = lax.axis_index("ctx")
    squares = None
    for h in range(HEADS):
        mix = m_in[h * DV : (h + 1) * DV, :] + far_mix(h, rank, (3, 4), states, q_ref, li_ref)
        m_ref[h * DV : (h + 1) * DV, :] = mix
        sq = jnp.sum(mix * mix, axis=0, keepdims=True)
        squares = sq if squares is None else squares + sq
    for i in range(TOK // 128):
        ss_ref[i : i + 1, :] = squares[:, i * 128 : (i + 1) * 128]


def gain_kernel(m_ref, g_ref, t_ref):
    t_ref[...] = m_ref[...] * g_ref[...].astype(jnp.float32).T


def norm_kernel(m_ref, s0, s1, s2, s3, out_hbm, o_ref, sems):
    total = (s0[...] + s1[...]) + (s2[...] + s3[...])
    inv = lax.rsqrt(total / (H * DV) + 1e-06)
    copies = []
    for i in range(TOK // 128):
        x = (m_ref[:, i * 128 : (i + 1) * 128] * inv[i : i + 1, :]).astype(jnp.bfloat16)
        o_ref[i * 128 : (i + 1) * 128, :] = x.T
        rows = pl.ds(i * 128, 128)
        copies.append(pltpu.make_async_copy(o_ref.at[rows], out_hbm.at[rows], sems.at[i]))
        copies[-1].start()
    for copy in copies:
        copy.wait()


WHOLE = pl.BlockSpec(memory_space=pltpu.VMEM)
HBM = pl.BlockSpec(memory_space=pltpu.HBM)


def call(
    kernel,
    outs,
    n_in,
    name,
    flops=0,
    moved=0,
    in_specs=None,
    out_specs=None,
    scratch=(),
    grid=(),
    vmem=VMEM_LIMIT,
):
    return pl.pallas_call(
        kernel,
        grid=grid,
        out_shape=outs,
        in_specs=in_specs or [WHOLE] * n_in,
        out_specs=out_specs or jax.tree.map(lambda _: WHOLE, outs),
        scratch_shapes=scratch,
        compiler_params=pltpu.CompilerParams(vmem_limit_bytes=vmem),
        cost_estimate=pl.CostEstimate(flops=flops, bytes_accessed=moved, transcendentals=0),
        name=name,
    )


def f32(*shape):
    return jax.ShapeDtypeStruct(shape, jnp.float32)


def in_hbm(x):
    return pltpu.with_memory_space_constraint(x, pltpu.HBM)


def bf16(*shape):
    return jax.ShapeDtypeStruct(shape, jnp.bfloat16)


def on_device(queries, keys, values, norm_gain, level_index):
    ctx = lax.axis_size("ctx")
    state = f32(PER * DV, DK)
    mixed = f32(HEADS * DV, TOK)

    def over_ctx(chunks, move):
        pairs = []
        for r in range(ctx):
            to = move(r // Z, r % Z)
            if to is not None:
                pairs.append((r, to[0] * Z + to[1]))
        return [lax.ppermute(x, "ctx", pairs) for x in chunks]

    def add(a, b):
        return [x + y for x, y in zip(a, b)]

    *own, keys_here, values_turned = call(
        summary_kernel,
        [state] * CHUNKS + [bf16(TOK, HEADS * DK), bf16(HEADS * DV, TOK)],
        2,
        "summary",
        268_000_000,
        3_200_000,
        in_specs=[HBM, HBM],
        scratch=[
            pltpu.VMEM((TOK, HEADS * DV), jnp.bfloat16),
            pltpu.SemaphoreType.DMA((2, TOK // SUM_BLK)),
        ],
    )(in_hbm(keys), in_hbm(values))

    half = HEADS // 2
    parts = []
    for p in range(2):
        parts.append(
            call(
                functools.partial(local_kernel, p * half, half),
                f32(half * DV, TOK),
                4,
                "local%d" % p,
                1_000_000_000,
                2_000_000,
                in_specs=[
                    pl.BlockSpec((TOK, half * DK), lambda i, p=p: (0, p)),
                    pl.BlockSpec((TOK, half * DK), lambda i, p=p: (0, p)),
                    pl.BlockSpec((half * DV, TOK), lambda i, p=p: (p, 0)),
                    pl.BlockSpec(level_index.shape, lambda i: (0, 0, 0)),
                ],
                out_specs=pl.BlockSpec((half * DV, TOK), lambda i: (0, 0)),
                grid=(1,),
            )(queries, keys_here, values_turned, level_index)
        )

    l0 = over_ctx(own, lambda y, z: (y, z ^ 1))
    l0[-1], parts[0] = lax.optimization_barrier((l0[-1], parts[0]))
    pair = add(own, l0)
    l1 = over_ctx(pair, lambda y, z: (y, z ^ 3))
    l1[-1], parts[1] = lax.optimization_barrier((l1[-1], parts[1]))
    quad = add(pair, l1)
    hop = (7, 6, 5, 4, 2, 3, 0, 1)
    l2 = over_ctx(quad, lambda y, z: (y, hop[z]))
    group = add(quad, l2)
    l3 = over_ctx(group, lambda y, z: (y ^ 1, z))
    up = [over_ctx(group, lambda y, z, k=k: (y ^ k, z)) for k in (3, 2)]
    near = call(
        functools.partial(far_kernel, (0, 1, 2)),
        mixed,
        4 + 3 * CHUNKS,
        "far012",
        268_000_000,
        3_000_000,
    )(queries, level_index, *l0, *l1, *l2, *parts)
    flat, squares = call(
        last_kernel, (mixed, f32(8, 128)), 3 + 3 * CHUNKS, "last", 67_000_000, 3_000_000
    )(queries, level_index, *l3, *up[0], *up[1], near)

    scaled = call(gain_kernel, mixed, 2, "gain", 1_000_000, 2_000_000)(
        flat, norm_gain.reshape(1, HEADS * DV)
    )
    def over_head(x, move):
        pairs = [(i, (i // 2, i % 2)) for i in range(8)]
        return lax.ppermute(
            x, "head", [(i, to[0] * 2 + to[1]) for i, to in ((i, move(*xc)) for i, xc in pairs)]
        )

    squares = squares + over_head(squares, lambda x, c: (x, 1 - c))
    one = over_head(squares, lambda x, c: (x ^ (1 if c == 0 else 3), 1 - c))
    two = over_head(squares, lambda x, c: (x ^ 2, c))
    three = over_head(one, lambda x, c: (x, 1 - c))
    others = (one, two, three)
    return call(
        norm_kernel,
        bf16(TOK, HEADS * DV),
        5,
        "norm",
        1_000_000,
        1_500_000,
        out_specs=HBM,
        scratch=[pltpu.VMEM((TOK, HEADS * DV), jnp.bfloat16), pltpu.SemaphoreType.DMA((8,))],
    )(scaled, squares, *others)


def solution(mesh):
    in_specs = (
        P("ctx", "head"),
        P("ctx", "head"),
        P("ctx", "head"),
        P("head"),
        P(None, "head", "ctx"),
    )
    out_specs = P("ctx", "head")
    return jax.shard_map(
        on_device, mesh=mesh, in_specs=in_specs, out_specs=out_specs, check_vma=False
    )
```

```python
import functools

import jax
import jax.numpy as jnp
from jax import lax
from jax.experimental import pallas as pl
from jax.experimental.pallas import tpu as pltpu
from jax.sharding import PartitionSpec as P

H = 32
DK = 128
DV = 64
STRETCH = 64
HEADS = 4
TOK = 1024
BLK = 256
SUM_BLK = 512
Z = 8
VMEM_LIMIT = 32 * 1024 * 1024
CHUNKS = 1
PER = HEADS // CHUNKS

NT = (((1,), (1,)), ((), ()))
NN = (((1,), (0,)), ((), ()))


def dot(a, b, dims):
    return lax.dot_general(a, b, dims, preferred_element_type=jnp.float32)


def weight_scale(level):
    span = STRETCH if level == 0 else STRETCH * 2 ** (level - 1)
    return float(span) ** (-0.5) / 256.0


def weight_row(li_ref, level, head, start, size):
    row = li_ref[level, head : head + 1, start : start + size]
    return row.astype(jnp.float32) * weight_scale(level)


def summary_kernel(k_hbm, v_hbm, *refs):
    outs, (k_ref, vt_ref, v_ref, sems) = refs[:CHUNKS], refs[CHUNKS:]
    copies = []
    for b in range(TOK // SUM_BLK):
        rows = pl.ds(b * SUM_BLK, SUM_BLK)
        pair = (
            pltpu.make_async_copy(v_hbm.at[rows], v_ref.at[rows], sems.at[0, b]),
            pltpu.make_async_copy(k_hbm.at[rows], k_ref.at[rows], sems.at[1, b]),
        )
        for copy in pair:
            copy.start()
        copies.append(pair)
    totals = [None] * HEADS
    for b in range(TOK // SUM_BLK):
        for copy in copies[b]:
            copy.wait()
        r0 = b * SUM_BLK
        vt = v_ref[r0 : r0 + SUM_BLK, :].T
        vt_ref[:, r0 : r0 + SUM_BLK] = vt
        for h in range(HEADS):
            part = dot(
                vt[h * DV : (h + 1) * DV, :], k_ref[r0 : r0 + SUM_BLK, h * DK : (h + 1) * DK], NN
            )
            totals[h] = part if b == 0 else totals[h] + part
    for h in range(HEADS):
        at = (h % PER) * DV
        outs[h // PER][at : at + DV, :] = totals[h]


def local_kernel(first_head, heads, q_ref, k_ref, vt_ref, li_ref, m_ref):
    lane = lax.broadcasted_iota(jnp.int32, (1, BLK), 1)
    t_stretch = lane // STRETCH
    row = lax.broadcasted_iota(jnp.int32, (BLK, BLK), 0)
    col = lax.broadcasted_iota(jnp.int32, (BLK, BLK), 1)
    causal = (row // STRETCH == col // STRETCH) & (row <= col)
    zero = jnp.zeros((), jnp.bfloat16)
    before = [None] * heads
    first_half = [None] * heads
    for b in range(TOK // BLK):
        r0 = b * BLK
        for h in range(heads):
            wh = first_head + h
            q = q_ref[r0 : r0 + BLK, h * DK : (h + 1) * DK]
            k = k_ref[r0 : r0 + BLK, h * DK : (h + 1) * DK]
            vt = vt_ref[h * DV : (h + 1) * DV, r0 : r0 + BLK]
            sums = dot(
                jnp.concatenate(
                    [
                        jnp.where(t_stretch == 0, vt, zero),
                        jnp.where(t_stretch == 2, vt, zero),
                        jnp.where(t_stretch < 2, vt, zero),
                        vt,
                    ],
                    axis=0,
                ),
                k,
                NN,
            )
            total = sums[3 * DV :]
            rows = [k, sums[: 3 * DV].astype(jnp.bfloat16)]
            if b % 2 == 1:
                rows.append(before[h].astype(jnp.bfloat16))
            if b >= 2:
                rows.append(first_half[h].astype(jnp.bfloat16))
            prod = dot(jnp.concatenate(rows, axis=0), q, NT)
            low = jnp.where(causal, prod[:BLK], 0.0).astype(jnp.bfloat16)
            mix = dot(vt, low, NN) * weight_row(li_ref, 0, wh, r0, BLK)
            part = [prod[BLK + i * DV : BLK + (i + 1) * DV] for i in range(len(rows) + 1)]
            near = jnp.where(
                t_stretch == 1, part[0], jnp.where(t_stretch == 3, part[1], 0.0)
            )
            mix = mix + near * weight_row(li_ref, 1, wh, r0, BLK)
            mix = mix + jnp.where(t_stretch >= 2, part[2], 0.0) * weight_row(
                li_ref, 2, wh, r0, BLK
            )
            at = 3
            if b % 2 == 1:
                mix = mix + part[at] * weight_row(li_ref, 3, wh, r0, BLK)
                at += 1
            if b >= 2:
                mix = mix + part[at] * weight_row(li_ref, 4, wh, r0, BLK)
            m_ref[h * DV : (h + 1) * DV, r0 : r0 + BLK] = mix
            if b == 1:
                first_half[h] = before[h] + total
            before[h] = total


def far_mix(h, rank, bits, states, q_ref, li_ref):
    at = (h % PER) * DV
    rows = jnp.concatenate(
        [s[h // PER][at : at + DV, :].astype(jnp.bfloat16) for s in states], axis=0
    )
    prod = dot(rows, q_ref[:, h * DK : (h + 1) * DK], NT)
    mix = None
    for i, bit in enumerate(bits):
        has = (rank >> bit) & 1
        w = jnp.where(has == 1, weight_row(li_ref, 5 + bit, h, 0, TOK), 0.0)
        term = prod[i * DV : (i + 1) * DV] * w
        mix = term if mix is None else mix + term
    return mix


def grouped(refs, n):
    return [refs[i * CHUNKS : (i + 1) * CHUNKS] for i in range(n)]


def far_kernel(bits, q_ref, li_ref, *refs):
    n = len(bits) * CHUNKS
    states, m_in, m_ref = grouped(refs[:n], len(bits)), refs[n:-1], refs[-1]
    rank = lax.axis_index("ctx")
    per = HEADS // len(m_in)
    for h in range(HEADS):
        at = (h % per) * DV
        mix = far_mix(h, rank, bits, states, q_ref, li_ref)
        m_ref[h * DV : (h + 1) * DV, :] = m_in[h // per][at : at + DV, :] + mix


def last_kernel(q_ref, li_ref, *refs):
    l3, up3, up2 = grouped(refs[: 3 * CHUNKS], 3)
    m_in, m_ref, ss_ref = refs[3 * CHUNKS :]
    states = [l3, [a[...] + b[...] for a, b in zip(up3, up2)]]
    rank = lax.axis_index("ctx")
    squares = None
    for h in range(HEADS):
        mix = m_in[h * DV : (h + 1) * DV, :] + far_mix(h, rank, (3, 4), states, q_ref, li_ref)
        m_ref[h * DV : (h + 1) * DV, :] = mix
        sq = jnp.sum(mix * mix, axis=0, keepdims=True)
        squares = sq if squares is None else squares + sq
    for i in range(TOK // 128):
        ss_ref[i : i + 1, :] = squares[:, i * 128 : (i + 1) * 128]


def gain_kernel(m_ref, g_ref, t_ref):
    t_ref[...] = m_ref[...] * g_ref[...].astype(jnp.float32).T


def norm_kernel(m_ref, s0, s1, s2, s3, out_hbm, o_ref, sems):
    total = (s0[...] + s1[...]) + (s2[...] + s3[...])
    inv = lax.rsqrt(total / (H * DV) + 1e-06)
    copies = []
    for i in range(TOK // 128):
        x = (m_ref[:, i * 128 : (i + 1) * 128] * inv[i : i + 1, :]).astype(jnp.bfloat16)
        o_ref[i * 128 : (i + 1) * 128, :] = x.T
        rows = pl.ds(i * 128, 128)
        copies.append(pltpu.make_async_copy(o_ref.at[rows], out_hbm.at[rows], sems.at[i]))
        copies[-1].start()
    for copy in copies:
        copy.wait()


WHOLE = pl.BlockSpec(memory_space=pltpu.VMEM)
HBM = pl.BlockSpec(memory_space=pltpu.HBM)


def call(
    kernel,
    outs,
    n_in,
    name,
    flops=0,
    moved=0,
    in_specs=None,
    out_specs=None,
    scratch=(),
    grid=(),
    vmem=VMEM_LIMIT,
):
    return pl.pallas_call(
        kernel,
        grid=grid,
        out_shape=outs,
        in_specs=in_specs or [WHOLE] * n_in,
        out_specs=out_specs or jax.tree.map(lambda _: WHOLE, outs),
        scratch_shapes=scratch,
        compiler_params=pltpu.CompilerParams(vmem_limit_bytes=vmem),
        cost_estimate=pl.CostEstimate(flops=flops, bytes_accessed=moved, transcendentals=0),
        name=name,
    )


def f32(*shape):
    return jax.ShapeDtypeStruct(shape, jnp.float32)


def in_hbm(x):
    return pltpu.with_memory_space_constraint(x, pltpu.HBM)


def bf16(*shape):
    return jax.ShapeDtypeStruct(shape, jnp.bfloat16)


def on_device(queries, keys, values, norm_gain, level_index):
    ctx = lax.axis_size("ctx")
    state = f32(PER * DV, DK)
    mixed = f32(HEADS * DV, TOK)

    def over_ctx(chunks, move, other=None):
        moves = (move, other or move)
        pairs = []
        for r in range(ctx):
            for h in range(8):
                y, z = moves[h % 2](r // Z, r % Z)
                pairs.append((r * 8 + h, (y * Z + z) * 8 + h))
        return [lax.ppermute(x, ("ctx", "head"), pairs) for x in chunks]

    def add(a, b):
        return [x + y for x, y in zip(a, b)]

    *own, keys_here, values_turned = call(
        summary_kernel,
        [state] * CHUNKS + [bf16(TOK, HEADS * DK), bf16(HEADS * DV, TOK)],
        2,
        "summary",
        268_000_000,
        3_200_000,
        in_specs=[HBM, HBM],
        scratch=[
            pltpu.VMEM((TOK, HEADS * DV), jnp.bfloat16),
            pltpu.SemaphoreType.DMA((2, TOK // SUM_BLK)),
        ],
    )(in_hbm(keys), in_hbm(values))

    half = HEADS // 2
    parts = []
    for p in range(2):
        parts.append(
            call(
                functools.partial(local_kernel, p * half, half),
                f32(half * DV, TOK),
                4,
                "local%d" % p,
                1_000_000_000,
                2_000_000,
                in_specs=[
                    pl.BlockSpec((TOK, half * DK), lambda i, p=p: (0, p)),
                    pl.BlockSpec((TOK, half * DK), lambda i, p=p: (0, p)),
                    pl.BlockSpec((half * DV, TOK), lambda i, p=p: (p, 0)),
                    pl.BlockSpec(level_index.shape, lambda i: (0, 0, 0)),
                ],
                out_specs=pl.BlockSpec((half * DV, TOK), lambda i: (0, 0)),
                grid=(1,),
            )(queries, keys_here, values_turned, level_index)
        )

    l0 = over_ctx(own, lambda y, z: (y, z ^ 1))
    l0[-1], parts[0] = lax.optimization_barrier((l0[-1], parts[0]))
    pair = add(own, l0)
    l1 = over_ctx(pair, lambda y, z: (y, z ^ 3))
    l1[-1], parts[1] = lax.optimization_barrier((l1[-1], parts[1]))
    quad = add(pair, l1)
    hop = (7, 6, 5, 4, 2, 3, 0, 1)
    l2 = over_ctx(quad, lambda y, z: (y, hop[z]), lambda y, z: (y, 7 - z))
    group = add(quad, l2)
    l3 = over_ctx(group, lambda y, z: (y ^ 1, z))
    up = [over_ctx(group, lambda y, z, k=k: (y ^ k, z)) for k in (3, 2)]
    near = call(
        functools.partial(far_kernel, (0, 1, 2)),
        mixed,
        4 + 3 * CHUNKS,
        "far012",
        268_000_000,
        3_000_000,
    )(queries, level_index, *l0, *l1, *l2, *parts)
    flat, squares = call(
        last_kernel, (mixed, f32(8, 128)), 3 + 3 * CHUNKS, "last", 67_000_000, 3_000_000
    )(queries, level_index, *l3, *up[0], *up[1], near)

    scaled = call(gain_kernel, mixed, 2, "gain", 1_000_000, 2_000_000)(
        flat, norm_gain.reshape(1, HEADS * DV)
    )
    def over_head(x, move):
        pairs = [(i, (i // 2, i % 2)) for i in range(8)]
        return lax.ppermute(
            x, "head", [(i, to[0] * 2 + to[1]) for i, to in ((i, move(*xc)) for i, xc in pairs)]
        )

    squares = squares + over_head(squares, lambda x, c: (x, 1 - c))
    one = over_head(squares, lambda x, c: (x ^ (1 if c == 0 else 3), 1 - c))
    two = over_head(squares, lambda x, c: (x ^ 2, c))
    three = over_head(one, lambda x, c: (x, 1 - c))
    others = (one, two, three)
    return call(
        norm_kernel,
        bf16(TOK, HEADS * DV),
        5,
        "norm",
        1_000_000,
        1_500_000,
        out_specs=HBM,
        scratch=[pltpu.VMEM((TOK, HEADS * DV), jnp.bfloat16), pltpu.SemaphoreType.DMA((8,))],
    )(scaled, squares, *others)


def solution(mesh):
    in_specs = (
        P("ctx", "head"),
        P("ctx", "head"),
        P("ctx", "head"),
        P("head"),
        P(None, "head", "ctx"),
    )
    out_specs = P("ctx", "head")
    return jax.shard_map(
        on_device, mesh=mesh, in_specs=in_specs, out_specs=out_specs, check_vma=False
    )
```

```python
import functools

import jax
import jax.numpy as jnp
from jax import lax
from jax.experimental import pallas as pl
from jax.experimental.pallas import tpu as pltpu
from jax.sharding import PartitionSpec as P

H = 32
DK = 128
DV = 64
STRETCH = 64
HEADS = 4
TOK = 1024
BLK = 256
SUM_BLK = 512
Z = 8
VMEM_LIMIT = 32 * 1024 * 1024
CHUNKS = 1
PER = HEADS // CHUNKS

NT = (((1,), (1,)), ((), ()))
NN = (((1,), (0,)), ((), ()))


def dot(a, b, dims):
    return lax.dot_general(a, b, dims, preferred_element_type=jnp.float32)


def weight_scale(level):
    span = STRETCH if level == 0 else STRETCH * 2 ** (level - 1)
    return float(span) ** (-0.5) / 256.0


def weight_row(li_ref, level, head, start, size):
    row = li_ref[level, head : head + 1, start : start + size]
    return row.astype(jnp.float32) * weight_scale(level)


def summary_kernel(k_hbm, v_hbm, *refs):
    outs, (k_ref, vt_ref, v_ref, sems) = refs[:CHUNKS], refs[CHUNKS:]
    copies = []
    for b in range(TOK // SUM_BLK):
        rows = pl.ds(b * SUM_BLK, SUM_BLK)
        pair = (
            pltpu.make_async_copy(v_hbm.at[rows], v_ref.at[rows], sems.at[0, b]),
            pltpu.make_async_copy(k_hbm.at[rows], k_ref.at[rows], sems.at[1, b]),
        )
        for copy in pair:
            copy.start()
        copies.append(pair)
    totals = [None] * HEADS
    for b in range(TOK // SUM_BLK):
        for copy in copies[b]:
            copy.wait()
        r0 = b * SUM_BLK
        vt = v_ref[r0 : r0 + SUM_BLK, :].T
        vt_ref[:, r0 : r0 + SUM_BLK] = vt
        for h in range(HEADS):
            part = dot(
                vt[h * DV : (h + 1) * DV, :], k_ref[r0 : r0 + SUM_BLK, h * DK : (h + 1) * DK], NN
            )
            totals[h] = part if b == 0 else totals[h] + part
    for h in range(HEADS):
        at = (h % PER) * DV
        outs[h // PER][at : at + DV, :] = totals[h]


def local_kernel(first_head, heads, q_ref, k_ref, vt_ref, li_ref, m_ref):
    lane = lax.broadcasted_iota(jnp.int32, (1, BLK), 1)
    t_stretch = lane // STRETCH
    row = lax.broadcasted_iota(jnp.int32, (BLK, BLK), 0)
    col = lax.broadcasted_iota(jnp.int32, (BLK, BLK), 1)
    causal = (row // STRETCH == col // STRETCH) & (row <= col)
    zero = jnp.zeros((), jnp.bfloat16)
    before = [None] * heads
    first_half = [None] * heads
    for b in range(TOK // BLK):
        r0 = b * BLK
        for h in range(heads):
            wh = first_head + h
            q = q_ref[r0 : r0 + BLK, h * DK : (h + 1) * DK]
            k = k_ref[r0 : r0 + BLK, h * DK : (h + 1) * DK]
            vt = vt_ref[h * DV : (h + 1) * DV, r0 : r0 + BLK]
            sums = dot(
                jnp.concatenate(
                    [
                        jnp.where(t_stretch == 0, vt, zero),
                        jnp.where(t_stretch == 2, vt, zero),
                        jnp.where(t_stretch < 2, vt, zero),
                        vt,
                    ],
                    axis=0,
                ),
                k,
                NN,
            )
            total = sums[3 * DV :]
            rows = [k, sums[: 3 * DV].astype(jnp.bfloat16)]
            if b % 2 == 1:
                rows.append(before[h].astype(jnp.bfloat16))
            if b >= 2:
                rows.append(first_half[h].astype(jnp.bfloat16))
            prod = dot(jnp.concatenate(rows, axis=0), q, NT)
            low = jnp.where(causal, prod[:BLK], 0.0).astype(jnp.bfloat16)
            mix = dot(vt, low, NN) * weight_row(li_ref, 0, wh, r0, BLK)
            part = [prod[BLK + i * DV : BLK + (i + 1) * DV] for i in range(len(rows) + 1)]
            near = jnp.where(
                t_stretch == 1, part[0], jnp.where(t_stretch == 3, part[1], 0.0)
            )
            mix = mix + near * weight_row(li_ref, 1, wh, r0, BLK)
            mix = mix + jnp.where(t_stretch >= 2, part[2], 0.0) * weight_row(
                li_ref, 2, wh, r0, BLK
            )
            at = 3
            if b % 2 == 1:
                mix = mix + part[at] * weight_row(li_ref, 3, wh, r0, BLK)
                at += 1
            if b >= 2:
                mix = mix + part[at] * weight_row(li_ref, 4, wh, r0, BLK)
            m_ref[h * DV : (h + 1) * DV, r0 : r0 + BLK] = mix
            if b == 1:
                first_half[h] = before[h] + total
            before[h] = total


def far_mix(h, rank, bits, states, q_ref, li_ref):
    at = (h % PER) * DV
    rows = jnp.concatenate(
        [s[h // PER][at : at + DV, :].astype(jnp.bfloat16) for s in states], axis=0
    )
    prod = dot(rows, q_ref[:, h * DK : (h + 1) * DK], NT)
    mix = None
    for i, bit in enumerate(bits):
        has = (rank >> bit) & 1
        w = jnp.where(has == 1, weight_row(li_ref, 5 + bit, h, 0, TOK), 0.0)
        term = prod[i * DV : (i + 1) * DV] * w
        mix = term if mix is None else mix + term
    return mix


def grouped(refs, n):
    return [refs[i * CHUNKS : (i + 1) * CHUNKS] for i in range(n)]


def far_kernel(bits, q_ref, li_ref, *refs):
    n = len(bits) * CHUNKS
    states, m_in, m_ref = grouped(refs[:n], len(bits)), refs[n:-1], refs[-1]
    rank = lax.axis_index("ctx")
    per = HEADS // len(m_in)
    for h in range(HEADS):
        at = (h % per) * DV
        mix = far_mix(h, rank, bits, states, q_ref, li_ref)
        m_ref[h * DV : (h + 1) * DV, :] = m_in[h // per][at : at + DV, :] + mix


def last_kernel(q_ref, li_ref, *refs):
    l3, up3, up2 = grouped(refs[: 3 * CHUNKS], 3)
    m_in, m_ref, ss_ref = refs[3 * CHUNKS :]
    states = [l3, [a[...] + b[...] for a, b in zip(up3, up2)]]
    rank = lax.axis_index("ctx")
    squares = None
    for h in range(HEADS):
        mix = m_in[h * DV : (h + 1) * DV, :] + far_mix(h, rank, (3, 4), states, q_ref, li_ref)
        m_ref[h * DV : (h + 1) * DV, :] = mix
        sq = jnp.sum(mix * mix, axis=0, keepdims=True)
        squares = sq if squares is None else squares + sq
    for i in range(TOK // 128):
        ss_ref[i : i + 1, :] = squares[:, i * 128 : (i + 1) * 128]


def gain_kernel(m_ref, g_ref, t_ref):
    t_ref[...] = m_ref[...] * g_ref[...].astype(jnp.float32).T


def norm_kernel(m_ref, s0, s1, s2, s3, out_hbm, o_ref, sems):
    total = (s0[...] + s1[...]) + (s2[...] + s3[...])
    inv = lax.rsqrt(total / (H * DV) + 1e-06)
    copies = []
    for i in range(TOK // 128):
        x = (m_ref[:, i * 128 : (i + 1) * 128] * inv[i : i + 1, :]).astype(jnp.bfloat16)
        o_ref[i * 128 : (i + 1) * 128, :] = x.T
        rows = pl.ds(i * 128, 128)
        copies.append(pltpu.make_async_copy(o_ref.at[rows], out_hbm.at[rows], sems.at[i]))
        copies[-1].start()
    for copy in copies:
        copy.wait()


WHOLE = pl.BlockSpec(memory_space=pltpu.VMEM)
HBM = pl.BlockSpec(memory_space=pltpu.HBM)


def call(
    kernel,
    outs,
    n_in,
    name,
    flops=0,
    moved=0,
    in_specs=None,
    out_specs=None,
    scratch=(),
    grid=(),
    vmem=VMEM_LIMIT,
):
    return pl.pallas_call(
        kernel,
        grid=grid,
        out_shape=outs,
        in_specs=in_specs or [WHOLE] * n_in,
        out_specs=out_specs or jax.tree.map(lambda _: WHOLE, outs),
        scratch_shapes=scratch,
        compiler_params=pltpu.CompilerParams(vmem_limit_bytes=vmem),
        cost_estimate=pl.CostEstimate(flops=flops, bytes_accessed=moved, transcendentals=0),
        name=name,
    )


def f32(*shape):
    return jax.ShapeDtypeStruct(shape, jnp.float32)


def in_hbm(x):
    return pltpu.with_memory_space_constraint(x, pltpu.HBM)


def bf16(*shape):
    return jax.ShapeDtypeStruct(shape, jnp.bfloat16)


def on_device(queries, keys, values, norm_gain, level_index):
    ctx = lax.axis_size("ctx")
    state = f32(PER * DV, DK)
    mixed = f32(HEADS * DV, TOK)

    def over_ctx(chunks, move, other=None):
        moves = (move, other or move)
        pairs = []
        for r in range(ctx):
            for h in range(8):
                y, z = moves[h % 2](r // Z, r % Z)
                pairs.append((r * 8 + h, (y * Z + z) * 8 + h))
        return [lax.ppermute(x, ("ctx", "head"), pairs) for x in chunks]

    def add(a, b):
        return [x + y for x, y in zip(a, b)]

    *own, keys_here, values_turned = call(
        summary_kernel,
        [state] * CHUNKS + [bf16(TOK, HEADS * DK), bf16(HEADS * DV, TOK)],
        2,
        "summary",
        268_000_000,
        3_200_000,
        in_specs=[HBM, HBM],
        scratch=[
            pltpu.VMEM((TOK, HEADS * DV), jnp.bfloat16),
            pltpu.SemaphoreType.DMA((2, TOK // SUM_BLK)),
        ],
    )(in_hbm(keys), in_hbm(values))

    half = HEADS // 2
    parts = []
    for p in range(2):
        parts.append(
            call(
                functools.partial(local_kernel, p * half, half),
                f32(half * DV, TOK),
                4,
                "local%d" % p,
                1_000_000_000,
                2_000_000,
                in_specs=[
                    pl.BlockSpec((TOK, half * DK), lambda i, p=p: (0, p)),
                    pl.BlockSpec((TOK, half * DK), lambda i, p=p: (0, p)),
                    pl.BlockSpec((half * DV, TOK), lambda i, p=p: (p, 0)),
                    pl.BlockSpec(level_index.shape, lambda i: (0, 0, 0)),
                ],
                out_specs=pl.BlockSpec((half * DV, TOK), lambda i: (0, 0)),
                grid=(1,),
            )(queries, keys_here, values_turned, level_index)
        )

    l0 = over_ctx(own, lambda y, z: (y, z ^ 1))
    l0[-1], parts[0] = lax.optimization_barrier((l0[-1], parts[0]))
    pair = add(own, l0)
    l1 = over_ctx(pair, lambda y, z: (y, z ^ 3))
    l1[-1], parts[1] = lax.optimization_barrier((l1[-1], parts[1]))
    quad = add(pair, l1)
    hop = (7, 6, 5, 4, 2, 3, 0, 1)
    l2 = over_ctx(quad, lambda y, z: (y, hop[z]), lambda y, z: (y, 7 - z))
    group = add(quad, l2)
    l3 = over_ctx(group, lambda y, z: (y ^ 1, z))
    far = (2, 3, 1, 0)
    up = [over_ctx(group, lambda y, z: (y ^ 3, z)), over_ctx(group, lambda y, z: (far[y], z))]
    near = call(
        functools.partial(far_kernel, (0, 1, 2)),
        mixed,
        4 + 3 * CHUNKS,
        "far012",
        268_000_000,
        3_000_000,
    )(queries, level_index, *l0, *l1, *l2, *parts)
    flat, squares = call(
        last_kernel, (mixed, f32(8, 128)), 3 + 3 * CHUNKS, "last", 67_000_000, 3_000_000
    )(queries, level_index, *l3, *up[0], *up[1], near)

    scaled = call(gain_kernel, mixed, 2, "gain", 1_000_000, 2_000_000)(
        flat, norm_gain.reshape(1, HEADS * DV)
    )
    def over_head(x, move):
        pairs = [(i, (i // 2, i % 2)) for i in range(8)]
        return lax.ppermute(
            x, "head", [(i, to[0] * 2 + to[1]) for i, to in ((i, move(*xc)) for i, xc in pairs)]
        )

    squares = squares + over_head(squares, lambda x, c: (x, 1 - c))
    one = over_head(squares, lambda x, c: (x ^ (1 if c == 0 else 3), 1 - c))
    two = over_head(squares, lambda x, c: (x ^ 2, c))
    three = over_head(one, lambda x, c: (x, 1 - c))
    others = (one, two, three)
    return call(
        norm_kernel,
        bf16(TOK, HEADS * DV),
        5,
        "norm",
        1_000_000,
        1_500_000,
        out_specs=HBM,
        scratch=[pltpu.VMEM((TOK, HEADS * DV), jnp.bfloat16), pltpu.SemaphoreType.DMA((8,))],
    )(scaled, squares, *others)


def solution(mesh):
    in_specs = (
        P("ctx", "head"),
        P("ctx", "head"),
        P("ctx", "head"),
        P("head"),
        P(None, "head", "ctx"),
    )
    out_specs = P("ctx", "head")
    return jax.shard_map(
        on_device, mesh=mesh, in_specs=in_specs, out_specs=out_specs, check_vma=False
    )
```

```python
import functools

import jax
import jax.numpy as jnp
from jax import lax
from jax.experimental import pallas as pl
from jax.experimental.pallas import tpu as pltpu
from jax.sharding import PartitionSpec as P

H = 32
DK = 128
DV = 64
STRETCH = 64
HEADS = 4
TOK = 1024
BLK = 256
SUM_BLK = 512
Z = 8
VMEM_LIMIT = 32 * 1024 * 1024
CHUNKS = 1
PER = HEADS // CHUNKS

NT = (((1,), (1,)), ((), ()))
NN = (((1,), (0,)), ((), ()))


def dot(a, b, dims):
    return lax.dot_general(a, b, dims, preferred_element_type=jnp.float32)


def weight_scale(level):
    span = STRETCH if level == 0 else STRETCH * 2 ** (level - 1)
    return float(span) ** (-0.5) / 256.0


def weight_row(li_ref, level, head, start, size):
    row = li_ref[level, head : head + 1, start : start + size]
    return row.astype(jnp.float32) * weight_scale(level)


def summary_kernel(k_hbm, v_hbm, *refs):
    outs, (k_ref, vt_ref, v_ref, sems) = refs[:CHUNKS], refs[CHUNKS:]
    copies = []
    for b in range(TOK // SUM_BLK):
        rows = pl.ds(b * SUM_BLK, SUM_BLK)
        pair = (
            pltpu.make_async_copy(v_hbm.at[rows], v_ref.at[rows], sems.at[0, b]),
            pltpu.make_async_copy(k_hbm.at[rows], k_ref.at[rows], sems.at[1, b]),
        )
        for copy in pair:
            copy.start()
        copies.append(pair)
    totals = [None] * HEADS
    for b in range(TOK // SUM_BLK):
        for copy in copies[b]:
            copy.wait()
        r0 = b * SUM_BLK
        vt = v_ref[r0 : r0 + SUM_BLK, :].T
        vt_ref[:, r0 : r0 + SUM_BLK] = vt
        for h in range(HEADS):
            part = dot(
                vt[h * DV : (h + 1) * DV, :], k_ref[r0 : r0 + SUM_BLK, h * DK : (h + 1) * DK], NN
            )
            totals[h] = part if b == 0 else totals[h] + part
    for h in range(HEADS):
        at = (h % PER) * DV
        outs[h // PER][at : at + DV, :] = totals[h]


def local_kernel(first_head, heads, q_ref, k_ref, vt_ref, li_ref, m_ref):
    lane = lax.broadcasted_iota(jnp.int32, (1, BLK), 1)
    t_stretch = lane // STRETCH
    row = lax.broadcasted_iota(jnp.int32, (BLK, BLK), 0)
    col = lax.broadcasted_iota(jnp.int32, (BLK, BLK), 1)
    causal = (row // STRETCH == col // STRETCH) & (row <= col)
    zero = jnp.zeros((), jnp.bfloat16)
    before = [None] * heads
    first_half = [None] * heads
    for b in range(TOK // BLK):
        r0 = b * BLK
        for h in range(heads):
            wh = first_head + h
            q = q_ref[r0 : r0 + BLK, h * DK : (h + 1) * DK]
            k = k_ref[r0 : r0 + BLK, h * DK : (h + 1) * DK]
            vt = vt_ref[h * DV : (h + 1) * DV, r0 : r0 + BLK]
            sums = dot(
                jnp.concatenate(
                    [
                        jnp.where(t_stretch == 0, vt, zero),
                        jnp.where(t_stretch == 2, vt, zero),
                        jnp.where(t_stretch < 2, vt, zero),
                        vt,
                    ],
                    axis=0,
                ),
                k,
                NN,
            )
            total = sums[3 * DV :]
            rows = [k, sums[: 3 * DV].astype(jnp.bfloat16)]
            if b % 2 == 1:
                rows.append(before[h].astype(jnp.bfloat16))
            if b >= 2:
                rows.append(first_half[h].astype(jnp.bfloat16))
            prod = dot(jnp.concatenate(rows, axis=0), q, NT)
            low = jnp.where(causal, prod[:BLK], 0.0).astype(jnp.bfloat16)
            mix = dot(vt, low, NN) * weight_row(li_ref, 0, wh, r0, BLK)
            part = [prod[BLK + i * DV : BLK + (i + 1) * DV] for i in range(len(rows) + 1)]
            near = jnp.where(
                t_stretch == 1, part[0], jnp.where(t_stretch == 3, part[1], 0.0)
            )
            mix = mix + near * weight_row(li_ref, 1, wh, r0, BLK)
            mix = mix + jnp.where(t_stretch >= 2, part[2], 0.0) * weight_row(
                li_ref, 2, wh, r0, BLK
            )
            at = 3
            if b % 2 == 1:
                mix = mix + part[at] * weight_row(li_ref, 3, wh, r0, BLK)
                at += 1
            if b >= 2:
                mix = mix + part[at] * weight_row(li_ref, 4, wh, r0, BLK)
            m_ref[h * DV : (h + 1) * DV, r0 : r0 + BLK] = mix
            if b == 1:
                first_half[h] = before[h] + total
            before[h] = total


def far_mix(h, rank, bits, states, q_ref, li_ref):
    at = (h % PER) * DV
    rows = jnp.concatenate(
        [s[h // PER][at : at + DV, :].astype(jnp.bfloat16) for s in states], axis=0
    )
    prod = dot(rows, q_ref[:, h * DK : (h + 1) * DK], NT)
    mix = None
    for i, bit in enumerate(bits):
        has = (rank >> bit) & 1
        w = jnp.where(has == 1, weight_row(li_ref, 5 + bit, h, 0, TOK), 0.0)
        term = prod[i * DV : (i + 1) * DV] * w
        mix = term if mix is None else mix + term
    return mix


def grouped(refs, n):
    return [refs[i * CHUNKS : (i + 1) * CHUNKS] for i in range(n)]


def far_kernel(bits, q_ref, li_ref, *refs):
    n = len(bits) * CHUNKS
    states, m_in, m_ref = grouped(refs[:n], len(bits)), refs[n:-1], refs[-1]
    rank = lax.axis_index("ctx")
    per = HEADS // len(m_in)
    for h in range(HEADS):
        at = (h % per) * DV
        mix = far_mix(h, rank, bits, states, q_ref, li_ref)
        m_ref[h * DV : (h + 1) * DV, :] = m_in[h // per][at : at + DV, :] + mix


def last_kernel(q_ref, li_ref, *refs):
    l3, up3, up2 = grouped(refs[: 3 * CHUNKS], 3)
    m_in, m_ref, ss_ref = refs[3 * CHUNKS :]
    states = [l3, [a[...] + b[...] for a, b in zip(up3, up2)]]
    rank = lax.axis_index("ctx")
    squares = None
    for h in range(HEADS):
        mix = m_in[h * DV : (h + 1) * DV, :] + far_mix(h, rank, (3, 4), states, q_ref, li_ref)
        m_ref[h * DV : (h + 1) * DV, :] = mix
        sq = jnp.sum(mix * mix, axis=0, keepdims=True)
        squares = sq if squares is None else squares + sq
    for i in range(TOK // 128):
        ss_ref[i : i + 1, :] = squares[:, i * 128 : (i + 1) * 128]


def gain_kernel(m_ref, g_ref, t_ref):
    t_ref[...] = m_ref[...] * g_ref[...].astype(jnp.float32).T


def norm_kernel(m_ref, s0, s1, s2, s3, out_hbm, o_ref, sems):
    total = (s0[...] + s1[...]) + (s2[...] + s3[...])
    inv = lax.rsqrt(total / (H * DV) + 1e-06)
    copies = []
    for i in range(TOK // 128):
        x = (m_ref[:, i * 128 : (i + 1) * 128] * inv[i : i + 1, :]).astype(jnp.bfloat16)
        o_ref[i * 128 : (i + 1) * 128, :] = x.T
        rows = pl.ds(i * 128, 128)
        copies.append(pltpu.make_async_copy(o_ref.at[rows], out_hbm.at[rows], sems.at[i]))
        copies[-1].start()
    for copy in copies:
        copy.wait()


WHOLE = pl.BlockSpec(memory_space=pltpu.VMEM)
HBM = pl.BlockSpec(memory_space=pltpu.HBM)


def call(
    kernel,
    outs,
    n_in,
    name,
    flops=0,
    moved=0,
    in_specs=None,
    out_specs=None,
    scratch=(),
    grid=(),
    vmem=VMEM_LIMIT,
):
    return pl.pallas_call(
        kernel,
        grid=grid,
        out_shape=outs,
        in_specs=in_specs or [WHOLE] * n_in,
        out_specs=out_specs or jax.tree.map(lambda _: WHOLE, outs),
        scratch_shapes=scratch,
        compiler_params=pltpu.CompilerParams(vmem_limit_bytes=vmem),
        cost_estimate=pl.CostEstimate(flops=flops, bytes_accessed=moved, transcendentals=0),
        name=name,
    )


def f32(*shape):
    return jax.ShapeDtypeStruct(shape, jnp.float32)


def in_hbm(x):
    return pltpu.with_memory_space_constraint(x, pltpu.HBM)


def bf16(*shape):
    return jax.ShapeDtypeStruct(shape, jnp.bfloat16)


def on_device(queries, keys, values, norm_gain, level_index):
    ctx = lax.axis_size("ctx")
    state = f32(PER * DV, DK)
    mixed = f32(HEADS * DV, TOK)

    def over_ctx(chunks, move, other=None):
        moves = (move, other or move)
        pairs = []
        for r in range(ctx):
            for h in range(8):
                y, z = moves[h % 2](r // Z, r % Z)
                pairs.append((r * 8 + h, (y * Z + z) * 8 + h))
        return [lax.ppermute(x, ("ctx", "head"), pairs) for x in chunks]

    def add(a, b):
        return [x + y for x, y in zip(a, b)]

    *own, keys_here, values_turned = call(
        summary_kernel,
        [state] * CHUNKS + [bf16(TOK, HEADS * DK), bf16(HEADS * DV, TOK)],
        2,
        "summary",
        268_000_000,
        3_200_000,
        in_specs=[HBM, HBM],
        scratch=[
            pltpu.VMEM((TOK, HEADS * DV), jnp.bfloat16),
            pltpu.SemaphoreType.DMA((2, TOK // SUM_BLK)),
        ],
    )(in_hbm(keys), in_hbm(values))

    half = HEADS // 2
    parts = []
    for p in range(2):
        parts.append(
            call(
                functools.partial(local_kernel, p * half, half),
                f32(half * DV, TOK),
                4,
                "local%d" % p,
                1_000_000_000,
                2_000_000,
                in_specs=[
                    pl.BlockSpec((TOK, half * DK), lambda i, p=p: (0, p)),
                    pl.BlockSpec((TOK, half * DK), lambda i, p=p: (0, p)),
                    pl.BlockSpec((half * DV, TOK), lambda i, p=p: (p, 0)),
                    pl.BlockSpec(level_index.shape, lambda i: (0, 0, 0)),
                ],
                out_specs=pl.BlockSpec((half * DV, TOK), lambda i: (0, 0)),
                grid=(1,),
            )(queries, keys_here, values_turned, level_index)
        )

    l0 = over_ctx(own, lambda y, z: (y, z ^ 1))
    l0[-1], parts[0] = lax.optimization_barrier((l0[-1], parts[0]))
    pair = add(own, l0)
    l1 = over_ctx(pair, lambda y, z: (y, z ^ 3))
    l1[-1], parts[1] = lax.optimization_barrier((l1[-1], parts[1]))
    quad = add(pair, l1)
    hop = (7, 6, 4, 5, 2, 3, 0, 1)
    l2 = over_ctx(quad, lambda y, z: (y, hop[z]), lambda y, z: (y, 7 - z))
    group = add(quad, l2)
    l3 = over_ctx(group, lambda y, z: (y ^ 1, z))
    far = (2, 3, 1, 0)
    up = [over_ctx(group, lambda y, z: (y ^ 3, z)), over_ctx(group, lambda y, z: (far[y], z))]
    near = call(
        functools.partial(far_kernel, (0, 1, 2)),
        mixed,
        4 + 3 * CHUNKS,
        "far012",
        268_000_000,
        3_000_000,
    )(queries, level_index, *l0, *l1, *l2, *parts)
    flat, squares = call(
        last_kernel, (mixed, f32(8, 128)), 3 + 3 * CHUNKS, "last", 67_000_000, 3_000_000
    )(queries, level_index, *l3, *up[0], *up[1], near)

    scaled = call(gain_kernel, mixed, 2, "gain", 1_000_000, 2_000_000)(
        flat, norm_gain.reshape(1, HEADS * DV)
    )
    def over_head(x, move):
        pairs = [(i, (i // 2, i % 2)) for i in range(8)]
        return lax.ppermute(
            x, "head", [(i, to[0] * 2 + to[1]) for i, to in ((i, move(*xc)) for i, xc in pairs)]
        )

    squares = squares + over_head(squares, lambda x, c: (x, 1 - c))
    one = over_head(squares, lambda x, c: (x ^ (1 if c == 0 else 3), 1 - c))
    two = over_head(squares, lambda x, c: (x ^ 2, c))
    three = over_head(one, lambda x, c: (x, 1 - c))
    others = (one, two, three)
    return call(
        norm_kernel,
        bf16(TOK, HEADS * DV),
        5,
        "norm",
        1_000_000,
        1_500_000,
        out_specs=HBM,
        scratch=[pltpu.VMEM((TOK, HEADS * DV), jnp.bfloat16), pltpu.SemaphoreType.DMA((8,))],
    )(scaled, squares, *others)


def solution(mesh):
    in_specs = (
        P("ctx", "head"),
        P("ctx", "head"),
        P("ctx", "head"),
        P("head"),
        P(None, "head", "ctx"),
    )
    out_specs = P("ctx", "head")
    return jax.shard_map(
        on_device, mesh=mesh, in_specs=in_specs, out_specs=out_specs, check_vma=False
    )
```
